32 devices in a mesh: groups: 2 (over y), expert: 16 (over z, x, core), replica: 1.
Axes of the slice: x: 2, y: 2, z: 4, core: 2. Of those that a mesh axis runs over, the one named last changes fastest.
Arguments:
- tokens: bfloat16 [1024, 4096], P(('groups', 'expert'), 'replica'), parts along dimension 0, may hold values from -6 to 6
- down_proj: bfloat16 [4096, 1024], P('replica'), may hold values from -0.09375 to 0.09375
- up_proj: bfloat16 [1024, 4096], P(None, 'replica'), may hold values from -0.1875 to 0.1875
- gate_weight: bfloat16 [16, 1024, 1344], P('expert', None, 'replica'), may hold values from -0.1875 to 0.1875
- lift_weight: bfloat16 [16, 1024, 1344], P('expert', None, 'replica'), may hold values from -0.1875 to 0.1875
- drop_weight: bfloat16 [16, 1344, 1024], P('expert', 'replica'), may hold values from -0.15625 to 0.15625
- routes: int32 [1024, 8], P(('groups', 'expert', 'replica')), parts along dimension 0, may hold values from 0 to 15, all different within a row; in each aligned block of 32 rows (0 to 31, 32 to 63, ...) at most 32 rows name the same one
- route_scale: int32 [1024, 8], P(('groups', 'expert', 'replica')), parts along dimension 0, may hold values from 1 to 16
Outputs:
- mixed: bfloat16 [1024, 4096], P(('groups', 'expert'), 'replica'), parts along dimension 0
The draws below stay inside these ranges and needn't reach their ends.
There are 2 independent parts, one for each index of `groups`. The reference program is written for one: setup_inputs(seed, part) draws one part's arguments, and reference() takes and returns one part's arrays. A program takes and returns all parts, laid end to end along the dimension named above; an argument that names none is the same for every part. Nothing has to cross between parts.
Inputs may be any that keep to these rules, and one draw needn't show every extreme that they name: `routes`: each row names 8 different experts; among the 32 rows of one device, no expert is named by more than 32 of them.
All inputs are finite; a program needn't handle non-finite values.
Results may differ from the reference program's by a relative error of at most 0.015.
Values may be sent and summed in bfloat16 or wider, within the bound.
A program may use at most 64 MiB of HBM per device.

```python
import math
import jax
import jax.numpy as jnp
import numpy as np
from jax import lax

D = 4096
LATENT = 1024
FF = 1344
TOP = 8
ROW_DEV = 32
EXPERTS = 16
TOKENS = 512
CAP = 32
MAXROWS = 512


def touch_ends(array, own_key, least, top_value):
    shape = array.shape
    place = [jax.random.randint(jax.random.fold_in(own_key, axis), (), 0, shape[axis]) for axis in range(len(shape))]
    array = array.at[tuple(place)].set(least)
    longest = shape.index(max(shape))
    place[longest] = (place[longest] + 1) % shape[longest]
    return array.at[tuple(place)].set(top_value)


def block_scale(own_key, shape, shards, least, top_value):
    gain = 1.0
    for axis_at, parts in shards:
        draws = jax.random.uniform(jax.random.fold_in(jax.random.fold_in(own_key, 6), axis_at), (parts,), jnp.float32, least / len(shards), top_value / len(shards))
        gain = gain * jnp.repeat(jnp.exp(draws), shape[axis_at] // parts).reshape((-1,) + (1,) * (len(shape) - 1 - axis_at))
    return gain


def routed_block(rng, own, number, rows, count, top, limit, lean):
    ranking = jax.random.permutation(rng, count)
    crowded, usual = shares(count, rows * top, limit, lean, True), shares(count, rows * top, limit, lean, False)
    places = jnp.arange(count)

    def named(tallies, turn):
        used = int((tallies > 0).sum())
        fixed = max(1, used // 4)
        moved = fixed + (places - fixed + turn * (used - fixed)) % max(1, count - fixed)
        return jnp.zeros((count,), jnp.int32).at[ranking[jnp.where(places < fixed, places, moved)]].set(jnp.asarray(tallies, jnp.int32))

    tallies = jnp.where(number % 4 == 0, named(crowded, number // 4), named(usual, number - number // 4 - 1))
    mixed = jax.random.permutation(jax.random.fold_in(own, 3), count)
    giver, receiver = mixed[0:count // 2 * 2:2], mixed[1:count // 2 * 2:2]
    margin = jnp.minimum(tallies[giver] - 1, limit - tallies[receiver]) // 2
    margin = jnp.where((giver == ranking[0]) | (receiver == ranking[0]) | (tallies[receiver] == 0), 0, jnp.maximum(margin, 0))
    moved = jax.random.randint(jax.random.fold_in(own, 4), (count // 2,), 0, 1 << 20) % (margin + 1)
    tallies = tallies.at[giver].add(-moved).at[receiver].add(moved)
    members = jnp.searchsorted(jnp.cumsum(tallies), jnp.arange(rows * top), side="right").astype(jnp.int32)
    grid = members.reshape(top, rows).T
    grid = grid[jax.random.permutation(jax.random.fold_in(own, 1), rows)]
    turn = jax.random.randint(jax.random.fold_in(own, 2), (rows, 1), 0, top)
    return jnp.take_along_axis(grid, (jnp.arange(top)[None, :] + turn) % top, axis=1)


def shares(number_of, total, reach, skew, full):
    weights = [(1 << 20) // math.isqrt(grade ** skew) + 1 for grade in range(1, number_of + 1)]
    largest = reach if full else min(reach, max(-(-total // number_of), total * weights[0] // sum(weights)))
    least = 1 if total - largest >= number_of - 1 else 0
    holding, spare = [largest] + [least] * (number_of - 1), total - largest - least * (number_of - 1)
    while spare > 0:
        movable = [i for i in range(1, number_of) if holding[i] < largest] or [i for i in range(1, number_of) if holding[i] < reach]
        whole, left = sum([weights[i] for i in movable]), spare
        for i in movable:
            more = min(reach - holding[i], max(1, left * weights[i] // whole), spare)
            holding[i] = holding[i] + more
            spare = spare - more
    return np.array(holding)


def normal_values(own_key, dims, scale, most, pieces=(), held_as=jnp.bfloat16):
    array = scale * jax.random.normal(own_key, dims, jnp.float32)
    if pieces:
        array = array * block_scale(own_key, dims, pieces, -0.22, 0.18)
    return jnp.clip(array, -most, most).astype(held_as)


def setup_inputs(seed: int = 0, part: int = 0) -> dict:
    key_of = jax.random.split(jax.random.key(seed), 9)
    part_splits = jax.random.split(jax.random.fold_in(key_of[8], part), 9)
    tokens = normal_values(part_splits[0], (TOKENS, D), 1.0, 6.0, ((0, 16),))
    down_proj = normal_values(key_of[1], (D, LATENT), D ** -0.5, 0.09375)
    up_proj = normal_values(key_of[2], (LATENT, D), LATENT ** -0.5, 0.1875)
    gate_weight = normal_values(key_of[3], (EXPERTS, LATENT, FF), LATENT ** -0.5, 0.1875, ((0, 16),))
    lift_weight = normal_values(key_of[4], (EXPERTS, LATENT, FF), LATENT ** -0.5, 0.1875, ((0, 16),))
    drop_weight = normal_values(key_of[5], (EXPERTS, FF, LATENT), FF ** -0.5, 0.15625, ((0, 16),))
    routes_keys = jax.random.split(jax.random.fold_in(part_splits[6], 1), TOKENS // ROW_DEV)
    routes_turns = jax.random.permutation(jax.random.fold_in(part_splits[6], 3), TOKENS // ROW_DEV)
    routes = jax.vmap(lambda own, number: routed_block(jax.random.fold_in(part_splits[6], 2), own, number, ROW_DEV, EXPERTS, TOP, CAP, 2))(routes_keys, routes_turns).reshape((TOKENS, TOP))
    route_scale = touch_ends(jax.random.randint(part_splits[7], (TOKENS, TOP), 1, 17), jax.random.fold_in(part_splits[7], 1), 1, 16).astype(jnp.int32)
    return dict(tokens=tokens, down_proj=down_proj, up_proj=up_proj, gate_weight=gate_weight, lift_weight=lift_weight, drop_weight=drop_weight, routes=routes, route_scale=route_scale)


def reference(tokens, down_proj, up_proj, gate_weight, lift_weight, drop_weight, routes, route_scale):
    latent = jnp.dot(tokens, down_proj, preferred_element_type=jnp.float32).astype(jnp.bfloat16)
    scale_f = route_scale.astype(jnp.float32)
    share = scale_f / jnp.sum(scale_f, axis=1, keepdims=True)
    flat_routes = routes.reshape(-1)
    flat_share = share.reshape(-1)
    owner_row = (jnp.arange(TOKENS * TOP) // TOP).astype(jnp.int32)
    expert_ids = jnp.arange(EXPERTS).astype(jnp.int32)

    def visit(accum, items):
        gate_mat, lift_mat, drop_mat, which = items
        chosen = flat_routes == which
        picks = jnp.nonzero(chosen, size=MAXROWS, fill_value=0)[0].astype(jnp.int32)
        valid = jnp.arange(MAXROWS) < jnp.sum(chosen.astype(jnp.int32))
        owners = owner_row[picks]
        inputs = latent[owners]
        gate = jnp.dot(inputs, gate_mat, preferred_element_type=jnp.float32)
        lifted = jnp.dot(inputs, lift_mat, preferred_element_type=jnp.float32)
        hidden = (jax.nn.silu(gate) * lifted).astype(jnp.bfloat16)
        outcome = jnp.dot(hidden, drop_mat, preferred_element_type=jnp.float32).astype(jnp.bfloat16)
        weight = jnp.where(valid, flat_share[picks], jnp.float32(0.0))
        accum = accum.at[owners].add(weight[:, None] * outcome.astype(jnp.float32))
        return accum, None

    start = jnp.zeros((TOKENS, LATENT), jnp.float32)
    accum, unused = lax.scan(visit, start, (gate_weight, lift_weight, drop_weight, expert_ids))
    combined = accum.astype(jnp.bfloat16)
    return jnp.dot(combined, up_proj, preferred_element_type=jnp.float32).astype(jnp.bfloat16)
```

```python
import functools

import jax
import jax.numpy as jnp
from jax import lax
from jax.experimental import pallas as pl
from jax.experimental.pallas import tpu as pltpu
from jax.sharding import PartitionSpec as P

MESH = pl.DeviceIdType.MESH
LANES = 128
DOWN_PARTS = 8
UP_PARTS = 4


def flip(value, mask):
    out, bit = value, 1
    while bit <= mask:
        if mask & bit:
            out = out + bit * (1 - 2 * ((value // bit) % 2))
        bit *= 2
    return out


def moe_kernel(
    layers, tokens, down, up, gate, lift, drop, routes, scale, out,
    tok_v, down_v, up_v, gate_v, lift_v, drop_v, routes_v, scale_v, out_v,
    lat, part, pair_out, pair_in, side_out, side_in, side_keep, line_out, line_in,
    load_sem, down_sem, up_sem, out_sem,
    line_ag_s, line_ag_r, side_ag_s, side_ag_r, pair_ag_s, pair_ag_r,
    pair_rs_s, pair_rs_r, side_rs_s, side_rs_r, line_rs_s, line_rs_r,
):
    me = lax.axis_index("expert")
    plane, side, core = me // 4, (me // 2) % 2, me % 2
    rows, width = line_in.shape[1:]
    depth = tokens.shape[1] // DOWN_PARTS
    span = out.shape[1] // UP_PARTS

    def at(step, other_side=0, other_core=0):
        x = 1 - side if other_side else side
        c = 1 - core if other_core else core
        return (flip(plane, step) * 2 + x) * 2 + c

    pair_peer, side_peer = at(0, 0, 1), at(0, 1, 0)
    line_peer = [at(step) for step in range(layers)]

    def send(src, dst, send_sem, recv_sem, peer):
        return pltpu.make_async_remote_copy(
            src_ref=src, dst_ref=dst, send_sem=send_sem, recv_sem=recv_sem,
            device_id={"expert": peer}, device_id_type=MESH,
        )

    loads = {
        name: pltpu.make_async_copy(src, dst, load_sem.at[i])
        for i, (name, src, dst) in enumerate((
            ("routes", routes, routes_v), ("scale", scale, scale_v), ("tokens", tokens, tok_v),
            ("gate", gate.at[0], gate_v), ("lift", lift.at[0], lift_v), ("drop", drop.at[0], drop_v),
        ))
    }
    down_loads = [
        pltpu.make_async_copy(down.at[pl.ds(k * depth, depth)], down_v.at[pl.ds(k * depth, depth)], down_sem.at[k])
        for k in range(DOWN_PARTS)
    ]
    up_loads = [
        pltpu.make_async_copy(up.at[:, pl.ds(k * span, span)], up_v.at[:, pl.ds(k * span, span)], up_sem.at[k])
        for k in range(UP_PARTS)
    ]
    loads["routes"].start()
    loads["scale"].start()
    loads["tokens"].start()
    for copy in down_loads:
        copy.start()

    barrier = pltpu.get_barrier_semaphore()
    peers = [pair_peer, side_peer] + line_peer[1:]
    for peer in peers:
        pl.semaphore_signal(barrier, inc=1, device_id={"expert": peer}, device_id_type=MESH)

    loads["routes"].wait()
    loads["scale"].wait()
    named, amount = routes_v[...], scale_v[...]
    lane = lax.broadcasted_iota(jnp.int32, (rows, LANES), 1)
    dense = jnp.zeros((rows, LANES), jnp.int32)
    for k in range(named.shape[1]):
        dense = dense + jnp.where(lane == named[:, k:k + 1], amount[:, k:k + 1], 0)
    lat[me, :, pl.ds(width, LANES)] = dense.astype(jnp.float32).astype(jnp.bfloat16)

    loads["tokens"].wait()
    total = jnp.zeros((rows, width), jnp.float32)
    later = {1: [loads["gate"]], 2: [loads["lift"]], 4: [loads["drop"]], 5: up_loads[:2], 6: up_loads[2:]}
    for k in range(DOWN_PARTS):
        down_loads[k].wait()
        for copy in later.get(k, []):
            copy.start()
        total = total + jnp.dot(
            tok_v[:, k * depth:(k + 1) * depth], down_v[k * depth:(k + 1) * depth, :],
            preferred_element_type=jnp.float32,
        )
    lat[me, :, pl.ds(0, width)] = total.astype(jnp.bfloat16)
    pl.semaphore_wait(barrier, len(peers))

    sent = []

    def go(copy):
        copy.start()
        sent.append(copy)

    def line_ag(step):
        return send(lat.at[me], lat.at[me], line_ag_s.at[step], line_ag_r.at[step], line_peer[step])

    def side_ag(step):
        slot = lat.at[at(step)]
        return send(slot, slot, side_ag_s.at[step], side_ag_r.at[step], side_peer)

    def pair_ag(step, other):
        slot, i = lat.at[at(step, other)], 2 * step + other
        return send(slot, slot, pair_ag_s.at[i], pair_ag_r.at[i], pair_peer)

    def got(slot, send_sem, recv_sem):
        send(lat.at[slot], lat.at[slot], send_sem, recv_sem, pair_peer).wait_recv()

    def from_line(step):
        got(at(step), line_ag_s.at[step], line_ag_r.at[step])
        go(side_ag(step))
        go(pair_ag(step, 0))

    def from_side(step):
        got(at(step, 1), side_ag_s.at[step], side_ag_r.at[step])
        go(pair_ag(step, 1))

    def from_pair(step):
        for other in range(2):
            i = 2 * step + other
            got(at(step, other, 1), pair_ag_s.at[i], pair_ag_r.at[i])

    def expert(step):
        first = flip(plane, step) * 4
        stacked = lat[pl.ds(first, 4), :, pl.ds(0, width)].reshape(4 * rows, width)
        gated = jnp.dot(stacked, gate_v[...], preferred_element_type=jnp.float32)
        lifted = jnp.dot(stacked, lift_v[...], preferred_element_type=jnp.float32)
        hidden = (gated / (1.0 + jnp.exp(-gated)) * lifted).astype(jnp.bfloat16)
        value = jnp.dot(hidden, drop_v[...], preferred_element_type=jnp.float32)
        weights = lat[pl.ds(first, 4), :, pl.ds(width, LANES)].reshape(4 * rows, LANES).astype(jnp.float32)
        lanes = lax.broadcasted_iota(jnp.int32, weights.shape, 1)
        mine = jnp.sum(jnp.where(lanes == me, weights, 0.0), axis=1, keepdims=True)
        part[step] = (value * mine).reshape(4, rows, width)
        for x in range(2):
            pair_out[step, x] = part[step, 2 * x + 1 - core].astype(jnp.bfloat16)
        go(send(pair_out.at[step], pair_in.at[step], pair_rs_s.at[step], pair_rs_r.at[step], pair_peer))

    def to_side(step):
        send(pair_out.at[step], pair_in.at[step], pair_rs_s.at[step], pair_rs_r.at[step], pair_peer).wait_recv()
        away = part[step, 2 * (1 - side) + core] + pair_in[step, 1 - side].astype(jnp.float32)
        side_out[step] = away.astype(jnp.bfloat16)
        go(send(side_out.at[step], side_in.at[step], side_rs_s.at[step], side_rs_r.at[step], side_peer))
        side_keep[step] = part[step, 2 * side + core] + pair_in[step, side].astype(jnp.float32)

    def to_line(step):
        send(side_out.at[step], side_in.at[step], side_rs_s.at[step], side_rs_r.at[step], side_peer).wait_recv()
        both = side_keep[step] + side_in[step].astype(jnp.float32)
        if step == 0:
            side_keep[0] = both
        else:
            line_out[step] = both.astype(jnp.bfloat16)
            go(send(line_out.at[step], line_in.at[step], line_rs_s.at[step], line_rs_r.at[step], line_peer[step]))

    for step in range(layers - 1, 0, -1):
        go(line_ag(step))
    go(side_ag(0))
    go(pair_ag(0, 0))
    if layers > 1:
        from_line(1)
    from_side(0)
    from_pair(0)
    loads["gate"].wait()
    loads["lift"].wait()
    loads["drop"].wait()
    for step in range(layers):
        expert(step)
        for ahead in (range(2, layers) if step == 0 else ()):
            from_line(ahead)
        if step + 1 < layers:
            from_side(step + 1)
            from_pair(step + 1)
        if step >= 1:
            to_side(step - 1)
        if step >= 2:
            to_line(step - 2)
    to_side(layers - 1)
    for step in range(max(0, layers - 2), layers):
        to_line(step)

    gathered = side_keep[0]
    for step in range(1, layers):
        send(line_out.at[step], line_in.at[step], line_rs_s.at[step], line_rs_r.at[step], line_peer[step]).wait_recv()
        gathered = gathered + line_in[step].astype(jnp.float32)
    whole = jnp.sum(amount.astype(jnp.float32), axis=1, keepdims=True)
    combined = (gathered / whole).astype(jnp.bfloat16)
    stores = []
    for k in range(UP_PARTS):
        up_loads[k].wait()
        columns = pl.ds(k * span, span)
        out_v[:, columns] = jnp.dot(
            combined, up_v[:, columns], preferred_element_type=jnp.float32
        ).astype(jnp.bfloat16)
        copy = pltpu.make_async_copy(out_v.at[:, columns], out.at[:, columns], out_sem.at[k])
        copy.start()
        stores.append(copy)
    for copy in sent:
        copy.wait_send()
    for copy in stores:
        copy.wait()


def per_device_line(tokens, down_proj, up_proj, gate_weight, lift_weight, drop_weight, routes, route_scale):
    experts = lax.axis_size("expert")
    layers = experts // 4
    rows, width = tokens.shape[0], down_proj.shape[1]
    bf16, f32 = jnp.bfloat16, jnp.float32
    dma = pltpu.SemaphoreType.DMA
    hbm = pl.BlockSpec(memory_space=pl.ANY)
    return pl.pallas_call(
        functools.partial(moe_kernel, layers),
        out_shape=jax.ShapeDtypeStruct((rows, up_proj.shape[1]), bf16),
        in_specs=[hbm] * 8,
        out_specs=hbm,
        scratch_shapes=[
            pltpu.VMEM(tokens.shape, bf16),
            pltpu.VMEM(down_proj.shape, bf16),
            pltpu.VMEM(up_proj.shape, bf16),
            pltpu.VMEM(gate_weight.shape[1:], bf16),
            pltpu.VMEM(lift_weight.shape[1:], bf16),
            pltpu.VMEM(drop_weight.shape[1:], bf16),
            pltpu.VMEM(routes.shape, jnp.int32),
            pltpu.VMEM(route_scale.shape, jnp.int32),
            pltpu.VMEM((rows, up_proj.shape[1]), bf16),
            pltpu.VMEM((experts, rows, width + LANES), bf16),
            pltpu.VMEM((layers, 4, rows, width), f32),
            pltpu.VMEM((layers, 2, rows, width), bf16),
            pltpu.VMEM((layers, 2, rows, width), bf16),
            pltpu.VMEM((layers, rows, width), bf16),
            pltpu.VMEM((layers, rows, width), bf16),
            pltpu.VMEM((layers, rows, width), f32),
            pltpu.VMEM((layers, rows, width), bf16),
            pltpu.VMEM((layers, rows, width), bf16),
            dma((6,)), dma((DOWN_PARTS,)), dma((UP_PARTS,)), dma((UP_PARTS,)),
            dma((layers,)), dma((layers,)), dma((layers,)), dma((layers,)),
            dma((2 * layers,)), dma((2 * layers,)),
            dma((layers,)), dma((layers,)), dma((layers,)), dma((layers,)), dma((layers,)), dma((layers,)),
        ],
        compiler_params=pltpu.CompilerParams(
            collective_id=0, has_side_effects=True, vmem_limit_bytes=56 * 1024 * 1024
        ),
    )(tokens, down_proj, up_proj, gate_weight, lift_weight, drop_weight, routes, route_scale)


def expert_apply(inputs, gate_weight, lift_weight, drop_weight):
    width = inputs.shape[-1]
    stacked = inputs.reshape(-1, width)
    gate = jnp.dot(stacked, gate_weight[0], preferred_element_type=jnp.float32)
    lifted = jnp.dot(stacked, lift_weight[0], preferred_element_type=jnp.float32)
    hidden = (jax.nn.silu(gate) * lifted).astype(jnp.bfloat16)
    partial_value = jnp.dot(hidden, drop_weight[0], preferred_element_type=jnp.float32)
    return partial_value.reshape(inputs.shape[:-1] + (drop_weight.shape[-1],))


def per_device(
    tokens, down_proj, up_proj, gate_weight, lift_weight, drop_weight, routes, route_scale
):
    paired = lax.axis_size("replica")
    own_rows = tokens.shape[0] // paired
    latent = lax.psum_scatter(
        jnp.dot(tokens, down_proj, preferred_element_type=jnp.float32),
        "replica",
        scatter_dimension=0,
        tiled=True,
    ).astype(jnp.bfloat16)
    width = latent.shape[1]
    experts = gate_weight.shape[0] * lax.axis_size("expert")
    chosen_count = routes.shape[1]
    routed = own_rows * chosen_count
    capacity = min(own_rows, 2 * own_rows * chosen_count // experts)
    flat_routes = routes.reshape(-1)
    onehot = (flat_routes[:, None] == jnp.arange(experts)[None, :]).astype(jnp.float32)
    position = jnp.arange(routed)
    earlier_mask = (position[None, :] < position[:, None]).astype(jnp.float32)
    earlier = jnp.dot(earlier_mask, onehot, precision=lax.Precision.HIGHEST)
    slots = jnp.sum(earlier * onehot, axis=1).astype(jnp.int32)
    target = flat_routes * capacity + slots
    outgoing = jnp.zeros((experts * capacity, width), jnp.bfloat16)
    outgoing = outgoing.at[target].set(latent[position // chosen_count])
    outgoing = outgoing.reshape(experts, capacity, width)
    doubled = jnp.broadcast_to(outgoing[:, None], (experts, paired, capacity, width))
    doubled = doubled.reshape(experts * paired, capacity, width)
    partial_value = expert_apply(
        lax.all_to_all(doubled, ("expert", "replica"), split_axis=0, concat_axis=0, tiled=True),
        gate_weight,
        lift_weight,
        drop_weight,
    )
    partial_value = partial_value.reshape(experts, paired, capacity, width)
    halved = lax.psum_scatter(partial_value, "replica", scatter_dimension=1, tiled=True)
    outcome_local = halved.reshape(experts, capacity, width).astype(jnp.bfloat16)
    returned = lax.all_to_all(outcome_local, "expert", split_axis=0, concat_axis=0, tiled=True)
    picked = returned.reshape(experts * capacity, width)[target]
    scale_f = route_scale.astype(jnp.float32)
    share = scale_f / jnp.sum(scale_f, axis=1, keepdims=True)
    picked = picked.reshape(own_rows, chosen_count, width).astype(jnp.float32)
    combined = jnp.einsum("rk,rkl->rl", share, picked).astype(jnp.bfloat16)
    return jnp.dot(
        lax.all_gather(combined, "replica", axis=0, tiled=True),
        up_proj,
        preferred_element_type=jnp.float32,
    ).astype(jnp.bfloat16)


def solution(mesh):
    in_specs = (
        P(("groups", "expert"), "replica"),
        P("replica", None),
        P(None, "replica"),
        P("expert", None, "replica"),
        P("expert", None, "replica"),
        P("expert", "replica", None),
        P(("groups", "expert", "replica"), None),
        P(("groups", "expert", "replica"), None),
    )
    out_specs = P(("groups", "expert"), "replica")
    experts, paired = mesh.shape["expert"], mesh.shape["replica"]
    layers = experts // 4
    in_line = paired == 1 and experts == 4 * layers and layers & (layers - 1) == 0
    return jax.shard_map(
        per_device_line if in_line else per_device, mesh=mesh, in_specs=in_specs, out_specs=out_specs, check_vma=False
    )
```

```python
import functools

import jax
import jax.numpy as jnp
from jax import lax
from jax.experimental import pallas as pl
from jax.experimental.pallas import tpu as pltpu
from jax.sharding import PartitionSpec as P

MESH = pl.DeviceIdType.MESH
LANES = 128
DOWN_PARTS = 4
UP_PARTS = 4
LAST = (((1,), (1,)), ((), ()))


def flip(value, mask):
    out, bit = value, 1
    while bit <= mask:
        if mask & bit:
            out = out + bit * (1 - 2 * ((value // bit) % 2))
        bit *= 2
    return out


def moe_kernel(
    layers, tokens, down, up, gate, lift, drop, routes, scale, out,
    tok_v, down_v, up_v, gate_v, lift_v, drop_v, routes_v, scale_v, out_v,
    lat_0, lat_1, part, pair_out, pair_in, side_out, side_in, side_keep, line_out, line_in,
    load_sem, down_sem, up_sem, out_sem,
    line_ag_s, line_ag_r, side_ag_s, side_ag_r, pair_ag_s, pair_ag_r,
    pair_rs_s, pair_rs_r, side_rs_s, side_rs_r, line_rs_s, line_rs_r,
):
    me = lax.axis_index("expert")
    plane, side, core = me // 4, (me // 2) % 2, me % 2
    rows, half = line_in.shape[2:]
    depth = tokens.shape[1] // DOWN_PARTS
    span = out.shape[1] // UP_PARTS
    lat = (lat_0, lat_1)
    steps = range(layers)

    def at(step, other_side=0, other_core=0):
        x = 1 - side if other_side else side
        c = 1 - core if other_core else core
        return (flip(plane, step) * 2 + x) * 2 + c

    pair_peer, side_peer = at(0, 0, 1), at(0, 1, 0)
    line_peer = [at(step) for step in steps]

    def send(src, dst, send_sem, recv_sem, peer):
        return pltpu.make_async_remote_copy(
            src_ref=src, dst_ref=dst, send_sem=send_sem, recv_sem=recv_sem,
            device_id={"expert": peer}, device_id_type=MESH,
        )

    def columns(q):
        return pl.ds(q * half, half)

    loads = {
        name: pltpu.make_async_copy(src, dst, load_sem.at[i])
        for i, (name, src, dst) in enumerate((
            ("routes", routes, routes_v), ("scale", scale, scale_v), ("tokens", tokens, tok_v),
            ("gate", gate.at[0], gate_v), ("lift", lift.at[0], lift_v), ("drop", drop.at[0], drop_v),
        ))
    }
    down_loads = []
    for q in range(2):
        for k in range(DOWN_PARTS):
            block = (pl.ds(k * depth, depth), columns(q))
            down_loads.append(pltpu.make_async_copy(down.at[block], down_v.at[block], down_sem.at[q, k]))
    up_loads = [
        pltpu.make_async_copy(up.at[:, pl.ds(k * span, span)], up_v.at[:, pl.ds(k * span, span)], up_sem.at[k])
        for k in range(UP_PARTS)
    ]
    loads["tokens"].start()
    for copy in down_loads[:2]:
        copy.start()
    loads["routes"].start()
    loads["scale"].start()
    for copy in down_loads[2:]:
        copy.start()

    barrier = pltpu.get_barrier_semaphore()
    peers = [pair_peer, side_peer] + line_peer[1:]
    for peer in peers:
        pl.semaphore_signal(barrier, inc=1, device_id={"expert": peer}, device_id_type=MESH)

    loads["routes"].wait()
    loads["scale"].wait()
    named, amount = jnp.transpose(routes_v[...]), jnp.transpose(scale_v[...])
    lane = lax.broadcasted_iota(jnp.int32, (rows, LANES), 1)
    dense = jnp.zeros((rows, LANES), jnp.int32)
    for k in range(named.shape[1]):
        dense = dense + jnp.where(lane == named[:, k:k + 1], amount[:, k:k + 1], 0)
    lat_0[me, :, pl.ds(half, LANES)] = dense.astype(jnp.float32).astype(jnp.bfloat16)

    sent = []

    def go(copy):
        copy.start()
        sent.append(copy)

    def forward(refs, step, other, q, i, peer):
        slot = lat[q].at[at(step, other)]
        go(send(slot, slot, refs[0].at[q, i], refs[1].at[q, i], peer))

    def got(slot, q, recv_sem, i):
        block = lat[q].at[slot]
        send(block, block, recv_sem.at[q, i], recv_sem.at[q, i], pair_peer).wait_recv()

    line_ag, side_ag, pair_ag = (line_ag_s, line_ag_r), (side_ag_s, side_ag_r), (pair_ag_s, pair_ag_r)

    def own(q):
        for step in steps[1:]:
            block = lat[q].at[me]
            go(send(block, block, line_ag_s.at[q, step], line_ag_r.at[q, step], line_peer[step]))
            if step == 1:
                forward(side_ag, 0, 0, q, 0, side_peer)
        forward(pair_ag, 0, 0, q, 0, pair_peer)

    def from_line(step, q):
        got(at(step), q, line_ag_r, step)
        forward(side_ag, step, 0, q, step, side_peer)
        forward(pair_ag, step, 0, q, 2 * step, pair_peer)

    def from_side(step, q):
        got(at(step, 1), q, side_ag_r, step)
        forward(pair_ag, step, 1, q, 2 * step + 1, pair_peer)

    def from_pair(step):
        for q in range(2):
            for other in range(2):
                got(at(step, other, 1), q, pair_ag_r, 2 * step + other)

    loads["tokens"].wait()
    later = {
        (0, 1): [loads["gate"]], (0, 2): [loads["lift"]], (1, 0): [loads["drop"]],
        (1, 1): up_loads[:2], (1, 2): up_loads[2:],
    }
    for q in range(2):
        total = jnp.zeros((rows, half), jnp.float32)
        for k in range(DOWN_PARTS):
            down_loads[q * DOWN_PARTS + k].wait()
            for copy in later.get((q, k), []):
                copy.start()
            total = total + jnp.dot(
                tok_v[:, k * depth:(k + 1) * depth],
                down_v[k * depth:(k + 1) * depth, q * half:(q + 1) * half],
                preferred_element_type=jnp.float32,
            )
        lat[q][me, :, pl.ds(0, half)] = total.astype(jnp.bfloat16)
        if q == 0:
            pl.semaphore_wait(barrier, len(peers))
        own(q)

    def inner(step):
        first = flip(plane, step) * 4
        stacked = jnp.concatenate(
            [ref[pl.ds(first, 4), :, pl.ds(0, half)].reshape(4 * rows, half) for ref in lat], axis=1
        )
        gated = lax.dot_general(stacked, gate_v[...], LAST, preferred_element_type=jnp.float32)
        lifted = lax.dot_general(stacked, lift_v[...], LAST, preferred_element_type=jnp.float32)
        return (gated / (1.0 + jnp.exp(-gated)) * lifted).astype(jnp.bfloat16)

    def outer(step, hidden):
        first = flip(plane, step) * 4
        weights = lat_0[pl.ds(first, 4), :, pl.ds(half, LANES)].reshape(4 * rows, LANES).astype(jnp.float32)
        lanes = lax.broadcasted_iota(jnp.int32, weights.shape, 1)
        mine = jnp.sum(jnp.where(lanes == me, weights, 0.0), axis=1, keepdims=True)
        for q in range(2):
            value = jnp.dot(hidden, drop_v[:, q * half:(q + 1) * half], preferred_element_type=jnp.float32)
            part[q, step] = (value * mine).reshape(4, rows, half)
            for x in range(2):
                pair_out[q, step, x] = part[q, step, 2 * x + 1 - core].astype(jnp.bfloat16)
            go(pair_rs(step, q))

    def pair_rs(step, q):
        return send(pair_out.at[q, step], pair_in.at[q, step], pair_rs_s.at[q, step], pair_rs_r.at[q, step], pair_peer)

    def side_rs(step, q):
        return send(side_out.at[q, step], side_in.at[q, step], side_rs_s.at[q, step], side_rs_r.at[q, step], side_peer)

    def line_rs(step, q):
        return send(
            line_out.at[q, step], line_in.at[q, step], line_rs_s.at[q, step], line_rs_r.at[q, step], line_peer[step]
        )

    def to_side(step, q):
        pair_rs(step, q).wait_recv()
        away = part[q, step, 2 * (1 - side) + core] + pair_in[q, step, 1 - side].astype(jnp.float32)
        side_out[q, step] = away.astype(jnp.bfloat16)
        go(side_rs(step, q))
        side_keep[q, step] = part[q, step, 2 * side + core] + pair_in[q, step, side].astype(jnp.float32)

    def to_line(step, q):
        side_rs(step, q).wait_recv()
        both = side_keep[q, step] + side_in[q, step].astype(jnp.float32)
        if step == 0:
            side_keep[q, 0] = both
        else:
            line_out[q, step] = both.astype(jnp.bfloat16)
            go(line_rs(step, q))

    from_line(1, 0)
    from_side(0, 0)
    from_line(2, 0)
    from_line(3, 0)
    from_line(1, 1)
    from_side(0, 1)
    from_side(1, 0)
    for name in ("gate", "lift", "drop"):
        loads[name].wait()
    from_pair(0)
    hidden = inner(0)
    from_line(2, 1)
    from_line(3, 1)
    from_side(1, 1)
    outer(0, hidden)
    from_side(2, 0)
    from_pair(1)
    hidden = inner(1)
    from_side(3, 0)
    to_side(0, 0)
    to_side(0, 1)
    from_side(2, 1)
    outer(1, hidden)
    from_side(3, 1)
    from_pair(2)
    hidden = inner(2)
    to_side(1, 0)
    to_side(1, 1)
    outer(2, hidden)
    to_line(0, 0)
    to_line(0, 1)
    from_pair(3)
    to_line(1, 0)
    hidden = inner(3)
    to_side(2, 0)
    to_side(2, 1)
    to_line(1, 1)
    outer(3, hidden)
    to_line(2, 0)
    to_side(3, 0)
    to_line(2, 1)
    to_side(3, 1)
    to_line(3, 0)
    to_line(3, 1)

    whole = jnp.sum(amount.astype(jnp.float32), axis=1, keepdims=True)
    combined = []
    for q in range(2):
        gathered = side_keep[q, 0]
        for step in steps[1:]:
            line_rs(step, q).wait_recv()
            gathered = gathered + line_in[q, step].astype(jnp.float32)
        combined.append((gathered / whole).astype(jnp.bfloat16))
    combined = jnp.concatenate(combined, axis=1)
    stores = []
    for k in range(UP_PARTS):
        up_loads[k].wait()
        block = pl.ds(k * span, span)
        out_v[:, block] = jnp.dot(
            combined, up_v[:, block], preferred_element_type=jnp.float32
        ).astype(jnp.bfloat16)
        copy = pltpu.make_async_copy(out_v.at[:, block], out.at[:, block], out_sem.at[k])
        copy.start()
        stores.append(copy)
    for copy in sent:
        copy.wait_send()
    for copy in stores:
        copy.wait()


def per_device_line(tokens, down_proj, up_proj, gate_weight, lift_weight, drop_weight, routes, route_scale):
    experts = lax.axis_size("expert")
    layers = experts // 4
    rows, half = tokens.shape[0], down_proj.shape[1] // 2
    bf16, f32 = jnp.bfloat16, jnp.float32
    gate_weight, lift_weight = jnp.swapaxes(gate_weight, 1, 2), jnp.swapaxes(lift_weight, 1, 2)
    routes, route_scale = routes.T, route_scale.T
    dma = pltpu.SemaphoreType.DMA
    hbm = pl.BlockSpec(memory_space=pl.ANY)
    return pl.pallas_call(
        functools.partial(moe_kernel, layers),
        out_shape=jax.ShapeDtypeStruct((rows, up_proj.shape[1]), bf16),
        in_specs=[hbm] * 8,
        out_specs=hbm,
        scratch_shapes=[
            pltpu.VMEM(tokens.shape, bf16),
            pltpu.VMEM(down_proj.shape, bf16),
            pltpu.VMEM(up_proj.shape, bf16),
            pltpu.VMEM(gate_weight.shape[1:], bf16),
            pltpu.VMEM(lift_weight.shape[1:], bf16),
            pltpu.VMEM(drop_weight.shape[1:], bf16),
            pltpu.VMEM(routes.shape, jnp.int32),
            pltpu.VMEM(route_scale.shape, jnp.int32),
            pltpu.VMEM((rows, up_proj.shape[1]), bf16),
            pltpu.VMEM((experts, rows, half + LANES), bf16),
            pltpu.VMEM((experts, rows, half), bf16),
            pltpu.VMEM((2, layers, 4, rows, half), f32),
            pltpu.VMEM((2, layers, 2, rows, half), bf16),
            pltpu.VMEM((2, layers, 2, rows, half), bf16),
            pltpu.VMEM((2, layers, rows, half), bf16),
            pltpu.VMEM((2, layers, rows, half), bf16),
            pltpu.VMEM((2, layers, rows, half), f32),
            pltpu.VMEM((2, layers, rows, half), bf16),
            pltpu.VMEM((2, layers, rows, half), bf16),
            dma((6,)), dma((2, DOWN_PARTS)), dma((UP_PARTS,)), dma((UP_PARTS,)),
            dma((2, layers)), dma((2, layers)), dma((2, layers)), dma((2, layers)),
            dma((2, 2 * layers)), dma((2, 2 * layers)),
            dma((2, layers)), dma((2, layers)), dma((2, layers)), dma((2, layers)), dma((2, layers)), dma((2, layers)),
        ],
        compiler_params=pltpu.CompilerParams(
            collective_id=0, has_side_effects=True, vmem_limit_bytes=56 * 1024 * 1024
        ),
    )(tokens, down_proj, up_proj, gate_weight, lift_weight, drop_weight, routes, route_scale)


def expert_apply(inputs, gate_weight, lift_weight, drop_weight):
    width = inputs.shape[-1]
    stacked = inputs.reshape(-1, width)
    gate = jnp.dot(stacked, gate_weight[0], preferred_element_type=jnp.float32)
    lifted = jnp.dot(stacked, lift_weight[0], preferred_element_type=jnp.float32)
    hidden = (jax.nn.silu(gate) * lifted).astype(jnp.bfloat16)
    partial_value = jnp.dot(hidden, drop_weight[0], preferred_element_type=jnp.float32)
    return partial_value.reshape(inputs.shape[:-1] + (drop_weight.shape[-1],))


def per_device(
    tokens, down_proj, up_proj, gate_weight, lift_weight, drop_weight, routes, route_scale
):
    paired = lax.axis_size("replica")
    own_rows = tokens.shape[0] // paired
    latent = lax.psum_scatter(
        jnp.dot(tokens, down_proj, preferred_element_type=jnp.float32),
        "replica",
        scatter_dimension=0,
        tiled=True,
    ).astype(jnp.bfloat16)
    width = latent.shape[1]
    experts = gate_weight.shape[0] * lax.axis_size("expert")
    chosen_count = routes.shape[1]
    routed = own_rows * chosen_count
    capacity = min(own_rows, 2 * own_rows * chosen_count // experts)
    flat_routes = routes.reshape(-1)
    onehot = (flat_routes[:, None] == jnp.arange(experts)[None, :]).astype(jnp.float32)
    position = jnp.arange(routed)
    earlier_mask = (position[None, :] < position[:, None]).astype(jnp.float32)
    earlier = jnp.dot(earlier_mask, onehot, precision=lax.Precision.HIGHEST)
    slots = jnp.sum(earlier * onehot, axis=1).astype(jnp.int32)
    target = flat_routes * capacity + slots
    outgoing = jnp.zeros((experts * capacity, width), jnp.bfloat16)
    outgoing = outgoing.at[target].set(latent[position // chosen_count])
    outgoing = outgoing.reshape(experts, capacity, width)
    doubled = jnp.broadcast_to(outgoing[:, None], (experts, paired, capacity, width))
    doubled = doubled.reshape(experts * paired, capacity, width)
    partial_value = expert_apply(
        lax.all_to_all(doubled, ("expert", "replica"), split_axis=0, concat_axis=0, tiled=True),
        gate_weight,
        lift_weight,
        drop_weight,
    )
    partial_value = partial_value.reshape(experts, paired, capacity, width)
    halved = lax.psum_scatter(partial_value, "replica", scatter_dimension=1, tiled=True)
    outcome_local = halved.reshape(experts, capacity, width).astype(jnp.bfloat16)
    returned = lax.all_to_all(outcome_local, "expert", split_axis=0, concat_axis=0, tiled=True)
    picked = returned.reshape(experts * capacity, width)[target]
    scale_f = route_scale.astype(jnp.float32)
    share = scale_f / jnp.sum(scale_f, axis=1, keepdims=True)
    picked = picked.reshape(own_rows, chosen_count, width).astype(jnp.float32)
    combined = jnp.einsum("rk,rkl->rl", share, picked).astype(jnp.bfloat16)
    return jnp.dot(
        lax.all_gather(combined, "replica", axis=0, tiled=True),
        up_proj,
        preferred_element_type=jnp.float32,
    ).astype(jnp.bfloat16)


def solution(mesh):
    in_specs = (
        P(("groups", "expert"), "replica"),
        P("replica", None),
        P(None, "replica"),
        P("expert", None, "replica"),
        P("expert", None, "replica"),
        P("expert", "replica", None),
        P(("groups", "expert", "replica"), None),
        P(("groups", "expert", "replica"), None),
    )
    out_specs = P(("groups", "expert"), "replica")
    experts, paired = mesh.shape["expert"], mesh.shape["replica"]
    in_line = paired == 1 and experts == 16
    return jax.shard_map(
        per_device_line if in_line else per_device, mesh=mesh, in_specs=in_specs, out_specs=out_specs, check_vma=False
    )
```

```python
import functools

import jax
import jax.numpy as jnp
from jax import lax
from jax.experimental import pallas as pl
from jax.experimental.pallas import tpu as pltpu
from jax.sharding import PartitionSpec as P

MESH = pl.DeviceIdType.MESH
LANES = 128
DOWN_PARTS = 4
UP_PARTS = 4
LAST = (((1,), (1,)), ((), ()))


def flip(value, mask):
    out, bit = value, 1
    while bit <= mask:
        if mask & bit:
            out = out + bit * (1 - 2 * ((value // bit) % 2))
        bit *= 2
    return out


def moe_kernel(
    layers, tokens, down, up, gate, lift, drop, routes, scale, out,
    tok_v, down_v, up_v, gate_v, lift_v, drop_v, routes_v, scale_v, out_v,
    lat_0, lat_1, part, pair_out, pair_in, side_out, side_in, side_keep, line_out, line_in,
    load_sem, down_sem, up_sem, out_sem,
    line_ag_s, line_ag_r, side_ag_s, side_ag_r, pair_ag_s, pair_ag_r,
    pair_rs_s, pair_rs_r, side_rs_s, side_rs_r, line_rs_s, line_rs_r,
):
    me = lax.axis_index("expert")
    plane, side, core = me // 4, (me // 2) % 2, me % 2
    rows, half = line_in.shape[2:]
    depth = tokens.shape[1] // DOWN_PARTS
    span = out.shape[1] // UP_PARTS
    lat = (lat_0, lat_1)
    steps = range(layers)

    def at(step, other_side=0, other_core=0):
        x = 1 - side if other_side else side
        c = 1 - core if other_core else core
        return (flip(plane, step) * 2 + x) * 2 + c

    pair_peer, side_peer = at(0, 0, 1), at(0, 1, 0)
    line_peer = [at(step) for step in steps]

    def send(src, dst, send_sem, recv_sem, peer):
        return pltpu.make_async_remote_copy(
            src_ref=src, dst_ref=dst, send_sem=send_sem, recv_sem=recv_sem,
            device_id={"expert": peer}, device_id_type=MESH,
        )

    def columns(q):
        return pl.ds(q * half, half)

    loads = {
        name: pltpu.make_async_copy(src, dst, load_sem.at[i])
        for i, (name, src, dst) in enumerate((
            ("routes", routes, routes_v), ("scale", scale, scale_v), ("tokens", tokens, tok_v),
            ("gate", gate.at[0], gate_v), ("lift", lift.at[0], lift_v), ("drop", drop.at[0], drop_v),
        ))
    }
    down_loads = []
    for q in range(2):
        for k in range(DOWN_PARTS):
            block = (pl.ds(k * depth, depth), columns(q))
            down_loads.append(pltpu.make_async_copy(down.at[block], down_v.at[block], down_sem.at[q, k]))
    up_loads = [
        pltpu.make_async_copy(up.at[:, pl.ds(k * span, span)], up_v.at[:, pl.ds(k * span, span)], up_sem.at[k])
        for k in range(UP_PARTS)
    ]
    loads["tokens"].start()
    for copy in down_loads[:2]:
        copy.start()
    loads["routes"].start()
    loads["scale"].start()
    for copy in down_loads[2:]:
        copy.start()

    barrier = pltpu.get_barrier_semaphore()
    peers = [pair_peer, side_peer] + line_peer[1:]
    for peer in peers:
        pl.semaphore_signal(barrier, inc=1, device_id={"expert": peer}, device_id_type=MESH)

    loads["routes"].wait()
    loads["scale"].wait()
    named, amount = jnp.transpose(routes_v[...]), jnp.transpose(scale_v[...])
    lane = lax.broadcasted_iota(jnp.int32, (rows, LANES), 1)
    dense = jnp.zeros((rows, LANES), jnp.int32)
    for k in range(named.shape[1]):
        dense = dense + jnp.where(lane == named[:, k:k + 1], amount[:, k:k + 1], 0)
    lat_0[me, :, pl.ds(half, LANES)] = dense.astype(jnp.float32).astype(jnp.bfloat16)

    sent = []

    def go(copy):
        copy.start()
        sent.append(copy)

    def forward(refs, step, other, q, i, peer):
        slot = lat[q].at[at(step, other)]
        go(send(slot, slot, refs[0].at[q, i], refs[1].at[q, i], peer))

    def got(slot, q, recv_sem, i):
        block = lat[q].at[slot]
        send(block, block, recv_sem.at[q, i], recv_sem.at[q, i], pair_peer).wait_recv()

    line_ag, side_ag, pair_ag = (line_ag_s, line_ag_r), (side_ag_s, side_ag_r), (pair_ag_s, pair_ag_r)

    def own(q):
        for step in steps[1:3]:
            block = lat[q].at[me]
            go(send(block, block, line_ag_s.at[q, step], line_ag_r.at[q, step], line_peer[step]))
            if step == 1:
                forward(side_ag, 0, 0, q, 0, side_peer)
        forward(pair_ag, 0, 0, q, 0, pair_peer)

    def far(q):
        block = lat[q].at[me]
        go(send(block, block, line_ag_s.at[q, 3], line_ag_r.at[q, 3], line_peer[3]))

    def from_line(step, q):
        got(at(step), q, line_ag_r, step)
        forward(side_ag, step, 0, q, step, side_peer)
        forward(pair_ag, step, 0, q, 2 * step, pair_peer)

    def from_side(step, q):
        got(at(step, 1), q, side_ag_r, step)
        forward(pair_ag, step, 1, q, 2 * step + 1, pair_peer)

    def from_pair(step):
        for q in range(2):
            for other in range(2):
                got(at(step, other, 1), q, pair_ag_r, 2 * step + other)

    loads["tokens"].wait()
    later = {
        (0, 1): [loads["gate"]], (0, 2): [loads["lift"]], (1, 0): [loads["drop"]],
        (1, 1): up_loads[:2], (1, 2): up_loads[2:],
    }
    for q in range(2):
        total = jnp.zeros((rows, half), jnp.float32)
        for k in range(DOWN_PARTS):
            down_loads[q * DOWN_PARTS + k].wait()
            for copy in later.get((q, k), []):
                copy.start()
            total = total + jnp.dot(
                tok_v[:, k * depth:(k + 1) * depth],
                down_v[k * depth:(k + 1) * depth, q * half:(q + 1) * half],
                preferred_element_type=jnp.float32,
            )
        lat[q][me, :, pl.ds(0, half)] = total.astype(jnp.bfloat16)
        if q == 0:
            pl.semaphore_wait(barrier, len(peers))
        own(q)

    def inner(step):
        first = flip(plane, step) * 4
        stacked = jnp.concatenate(
            [ref[pl.ds(first, 4), :, pl.ds(0, half)].reshape(4 * rows, half) for ref in lat], axis=1
        )
        gated = lax.dot_general(stacked, gate_v[...], LAST, preferred_element_type=jnp.float32)
        lifted = lax.dot_general(stacked, lift_v[...], LAST, preferred_element_type=jnp.float32)
        return (gated / (1.0 + jnp.exp(-gated)) * lifted).astype(jnp.bfloat16)

    def outer(step, hidden):
        first = flip(plane, step) * 4
        weights = lat_0[pl.ds(first, 4), :, pl.ds(half, LANES)].reshape(4 * rows, LANES).astype(jnp.float32)
        lanes = lax.broadcasted_iota(jnp.int32, weights.shape, 1)
        mine = jnp.sum(jnp.where(lanes == me, weights, 0.0), axis=1, keepdims=True)
        for q in range(2):
            value = jnp.dot(hidden, drop_v[:, q * half:(q + 1) * half], preferred_element_type=jnp.float32)
            part[q, step] = (value * mine).reshape(4, rows, half)
            for x in range(2):
                pair_out[q, step, x] = part[q, step, 2 * x + 1 - core].astype(jnp.bfloat16)
            go(pair_rs(step, q))

    def pair_rs(step, q):
        return send(pair_out.at[q, step], pair_in.at[q, step], pair_rs_s.at[q, step], pair_rs_r.at[q, step], pair_peer)

    def side_rs(step, q):
        return send(side_out.at[q, step], side_in.at[q, step], side_rs_s.at[q, step], side_rs_r.at[q, step], side_peer)

    def line_rs(step, q):
        return send(
            line_out.at[q, step], line_in.at[q, step], line_rs_s.at[q, step], line_rs_r.at[q, step], line_peer[step]
        )

    def to_side(step, q):
        pair_rs(step, q).wait_recv()
        away = part[q, step, 2 * (1 - side) + core] + pair_in[q, step, 1 - side].astype(jnp.float32)
        side_out[q, step] = away.astype(jnp.bfloat16)
        go(side_rs(step, q))
        side_keep[q, step] = part[q, step, 2 * side + core] + pair_in[q, step, side].astype(jnp.float32)

    def to_line(step, q):
        side_rs(step, q).wait_recv()
        both = side_keep[q, step] + side_in[q, step].astype(jnp.float32)
        if step == 0:
            side_keep[q, 0] = both
        else:
            line_out[q, step] = both.astype(jnp.bfloat16)
            go(line_rs(step, q))

    from_line(1, 0)
    far(0)
    from_side(0, 0)
    far(1)
    from_line(2, 0)
    from_line(1, 1)
    from_side(0, 1)
    from_side(1, 0)
    from_line(2, 1)
    for name in ("gate", "lift", "drop"):
        loads[name].wait()
    from_pair(0)
    hidden = inner(0)
    from_line(3, 0)
    from_line(3, 1)
    from_side(1, 1)
    outer(0, hidden)
    from_side(2, 0)
    from_pair(1)
    hidden = inner(1)
    from_side(3, 0)
    to_side(0, 0)
    to_side(0, 1)
    from_side(2, 1)
    outer(1, hidden)
    from_side(3, 1)
    from_pair(2)
    hidden = inner(2)
    to_side(1, 0)
    to_side(1, 1)
    outer(2, hidden)
    to_line(0, 0)
    to_line(0, 1)
    from_pair(3)
    to_line(1, 0)
    hidden = inner(3)
    to_side(2, 0)
    to_side(2, 1)
    to_line(1, 1)
    outer(3, hidden)
    to_line(2, 0)
    to_side(3, 0)
    to_line(2, 1)
    to_side(3, 1)
    to_line(3, 0)
    to_line(3, 1)

    whole = jnp.sum(amount.astype(jnp.float32), axis=1, keepdims=True)
    combined = []
    for q in range(2):
        gathered = side_keep[q, 0]
        for step in steps[1:]:
            line_rs(step, q).wait_recv()
            gathered = gathered + line_in[q, step].astype(jnp.float32)
        combined.append((gathered / whole).astype(jnp.bfloat16))
    combined = jnp.concatenate(combined, axis=1)
    stores = []
    for k in range(UP_PARTS):
        up_loads[k].wait()
        block = pl.ds(k * span, span)
        out_v[:, block] = jnp.dot(
            combined, up_v[:, block], preferred_element_type=jnp.float32
        ).astype(jnp.bfloat16)
        copy = pltpu.make_async_copy(out_v.at[:, block], out.at[:, block], out_sem.at[k])
        copy.start()
        stores.append(copy)
    for copy in sent:
        copy.wait_send()
    for copy in stores:
        copy.wait()


def per_device_line(tokens, down_proj, up_proj, gate_weight, lift_weight, drop_weight, routes, route_scale):
    experts = lax.axis_size("expert")
    layers = experts // 4
    rows, half = tokens.shape[0], down_proj.shape[1] // 2
    bf16, f32 = jnp.bfloat16, jnp.float32
    gate_weight, lift_weight = jnp.swapaxes(gate_weight, 1, 2), jnp.swapaxes(lift_weight, 1, 2)
    routes, route_scale = routes.T, route_scale.T
    dma = pltpu.SemaphoreType.DMA
    hbm = pl.BlockSpec(memory_space=pl.ANY)
    return pl.pallas_call(
        functools.partial(moe_kernel, layers),
        out_shape=jax.ShapeDtypeStruct((rows, up_proj.shape[1]), bf16),
        in_specs=[hbm] * 8,
        out_specs=hbm,
        scratch_shapes=[
            pltpu.VMEM(tokens.shape, bf16),
            pltpu.VMEM(down_proj.shape, bf16),
            pltpu.VMEM(up_proj.shape, bf16),
            pltpu.VMEM(gate_weight.shape[1:], bf16),
            pltpu.VMEM(lift_weight.shape[1:], bf16),
            pltpu.VMEM(drop_weight.shape[1:], bf16),
            pltpu.VMEM(routes.shape, jnp.int32),
            pltpu.VMEM(route_scale.shape, jnp.int32),
            pltpu.VMEM((rows, up_proj.shape[1]), bf16),
            pltpu.VMEM((experts, rows, half + LANES), bf16),
            pltpu.VMEM((experts, rows, half), bf16),
            pltpu.VMEM((2, layers, 4, rows, half), f32),
            pltpu.VMEM((2, layers, 2, rows, half), bf16),
            pltpu.VMEM((2, layers, 2, rows, half), bf16),
            pltpu.VMEM((2, layers, rows, half), bf16),
            pltpu.VMEM((2, layers, rows, half), bf16),
            pltpu.VMEM((2, layers, rows, half), f32),
            pltpu.VMEM((2, layers, rows, half), bf16),
            pltpu.VMEM((2, layers, rows, half), bf16),
            dma((6,)), dma((2, DOWN_PARTS)), dma((UP_PARTS,)), dma((UP_PARTS,)),
            dma((2, layers)), dma((2, layers)), dma((2, layers)), dma((2, layers)),
            dma((2, 2 * layers)), dma((2, 2 * layers)),
            dma((2, layers)), dma((2, layers)), dma((2, layers)), dma((2, layers)), dma((2, layers)), dma((2, layers)),
        ],
        compiler_params=pltpu.CompilerParams(
            collective_id=0, has_side_effects=True, vmem_limit_bytes=56 * 1024 * 1024
        ),
    )(tokens, down_proj, up_proj, gate_weight, lift_weight, drop_weight, routes, route_scale)


def expert_apply(inputs, gate_weight, lift_weight, drop_weight):
    width = inputs.shape[-1]
    stacked = inputs.reshape(-1, width)
    gate = jnp.dot(stacked, gate_weight[0], preferred_element_type=jnp.float32)
    lifted = jnp.dot(stacked, lift_weight[0], preferred_element_type=jnp.float32)
    hidden = (jax.nn.silu(gate) * lifted).astype(jnp.bfloat16)
    partial_value = jnp.dot(hidden, drop_weight[0], preferred_element_type=jnp.float32)
    return partial_value.reshape(inputs.shape[:-1] + (drop_weight.shape[-1],))


def per_device(
    tokens, down_proj, up_proj, gate_weight, lift_weight, drop_weight, routes, route_scale
):
    paired = lax.axis_size("replica")
    own_rows = tokens.shape[0] // paired
    latent = lax.psum_scatter(
        jnp.dot(tokens, down_proj, preferred_element_type=jnp.float32),
        "replica",
        scatter_dimension=0,
        tiled=True,
    ).astype(jnp.bfloat16)
    width = latent.shape[1]
    experts = gate_weight.shape[0] * lax.axis_size("expert")
    chosen_count = routes.shape[1]
    routed = own_rows * chosen_count
    capacity = min(own_rows, 2 * own_rows * chosen_count // experts)
    flat_routes = routes.reshape(-1)
    onehot = (flat_routes[:, None] == jnp.arange(experts)[None, :]).astype(jnp.float32)
    position = jnp.arange(routed)
    earlier_mask = (position[None, :] < position[:, None]).astype(jnp.float32)
    earlier = jnp.dot(earlier_mask, onehot, precision=lax.Precision.HIGHEST)
    slots = jnp.sum(earlier * onehot, axis=1).astype(jnp.int32)
    target = flat_routes * capacity + slots
    outgoing = jnp.zeros((experts * capacity, width), jnp.bfloat16)
    outgoing = outgoing.at[target].set(latent[position // chosen_count])
    outgoing = outgoing.reshape(experts, capacity, width)
    doubled = jnp.broadcast_to(outgoing[:, None], (experts, paired, capacity, width))
    doubled = doubled.reshape(experts * paired, capacity, width)
    partial_value = expert_apply(
        lax.all_to_all(doubled, ("expert", "replica"), split_axis=0, concat_axis=0, tiled=True),
        gate_weight,
        lift_weight,
        drop_weight,
    )
    partial_value = partial_value.reshape(experts, paired, capacity, width)
    halved = lax.psum_scatter(partial_value, "replica", scatter_dimension=1, tiled=True)
    outcome_local = halved.reshape(experts, capacity, width).astype(jnp.bfloat16)
    returned = lax.all_to_all(outcome_local, "expert", split_axis=0, concat_axis=0, tiled=True)
    picked = returned.reshape(experts * capacity, width)[target]
    scale_f = route_scale.astype(jnp.float32)
    share = scale_f / jnp.sum(scale_f, axis=1, keepdims=True)
    picked = picked.reshape(own_rows, chosen_count, width).astype(jnp.float32)
    combined = jnp.einsum("rk,rkl->rl", share, picked).astype(jnp.bfloat16)
    return jnp.dot(
        lax.all_gather(combined, "replica", axis=0, tiled=True),
        up_proj,
        preferred_element_type=jnp.float32,
    ).astype(jnp.bfloat16)


def solution(mesh):
    in_specs = (
        P(("groups", "expert"), "replica"),
        P("replica", None),
        P(None, "replica"),
        P("expert", None, "replica"),
        P("expert", None, "replica"),
        P("expert", "replica", None),
        P(("groups", "expert", "replica"), None),
        P(("groups", "expert", "replica"), None),
    )
    out_specs = P(("groups", "expert"), "replica")
    experts, paired = mesh.shape["expert"], mesh.shape["replica"]
    in_line = paired == 1 and experts == 16
    return jax.shard_map(
        per_device_line if in_line else per_device, mesh=mesh, in_specs=in_specs, out_specs=out_specs, check_vma=False
    )
```
